32 devices in a mesh: seq: 4 (over y, x), fsdp: 8 (over z, core).
Axes of the slice: x: 2, y: 2, z: 4, core: 2. Of those that a mesh axis runs over, the one named last changes fastest.
Arguments:
- tokens: bfloat16 [8, 512, 1024], P('fsdp', 'seq'), may hold values from -6 to 6
- attn_gain: float32 [1024], replicated, may hold values from 0.25 to 1.75
- w_query: bfloat16 [1024, 1024], P(('seq', 'fsdp')), may hold values from -0.1875 to 0.1875
- w_key: bfloat16 [1024, 1024], P(('seq', 'fsdp')), may hold values from -0.1875 to 0.1875
- value_weight: bfloat16 [1024, 2048], P(('seq', 'fsdp')), may hold values from -0.1875 to 0.1875
- w_gate: bfloat16 [1024, 2048], P(('seq', 'fsdp')), may hold values from -0.1875 to 0.1875
- w_beta: bfloat16 [1024, 8], P(('seq', 'fsdp')), may hold values from -0.1875 to 0.1875
- w_decay: bfloat16 [1024, 8], P(('seq', 'fsdp')), may hold values from -0.1875 to 0.1875
- conv_query: float32 [4, 1024], replicated, may hold values from -2 to 2
- conv_key: float32 [4, 1024], replicated, may hold values from -2 to 2
- conv_value: float32 [4, 2048], replicated, may hold values from -2 to 2
- decay_rate: float32 [8], replicated, may hold values from 0 to 1, as said below
- decay_bias: float32 [8], replicated, may hold values from -1 to 1
- out_gain: float32 [256], replicated, may hold values from 0.25 to 1.75
- w_out: bfloat16 [2048, 1024], P(('seq', 'fsdp')), may hold values from -0.125 to 0.125
- mlp_gain: float32 [1024], replicated, may hold values from 0.25 to 1.75
- w_mlp_gate: bfloat16 [1024, 2816], P(('seq', 'fsdp')), may hold values from -0.1875 to 0.1875
- w_up: bfloat16 [1024, 2816], P(('seq', 'fsdp')), may hold values from -0.1875 to 0.1875
- w_down: bfloat16 [2816, 1024], P(('seq', 'fsdp')), may hold values from -0.109375 to 0.109375
- cotangent: bfloat16 [8, 512, 1024], P('fsdp', 'seq'), may hold values from -6 to 6
Outputs:
- output: bfloat16 [8, 512, 1024], P('fsdp', 'seq')
- grad_tokens: float32 [8, 512, 1024], P('fsdp', 'seq')
- grad_attn_gain: float32 [1024], replicated
- grad_w_query: float32 [1024, 1024], P(('seq', 'fsdp'))
- grad_w_key: float32 [1024, 1024], P(('seq', 'fsdp'))
- grad_w_value: float32 [1024, 2048], P(('seq', 'fsdp'))
- grad_w_gate: float32 [1024, 2048], P(('seq', 'fsdp'))
- grad_w_beta: float32 [1024, 8], P(('seq', 'fsdp'))
- grad_w_decay: float32 [1024, 8], P(('seq', 'fsdp'))
- grad_conv_query: float32 [4, 1024], replicated
- grad_conv_key: float32 [4, 1024], replicated
- grad_conv_value: float32 [4, 2048], replicated
- grad_decay_rate: float32 [8], replicated
- grad_decay_bias: float32 [8], replicated
- grad_out_gain: float32 [256], replicated
- grad_w_out: float32 [2048, 1024], P(('seq', 'fsdp'))
- grad_mlp_gain: float32 [1024], replicated
- grad_w_mlp_gate: float32 [1024, 2816], P(('seq', 'fsdp'))
- grad_w_up: float32 [1024, 2816], P(('seq', 'fsdp'))
- grad_w_down: float32 [2816, 1024], P(('seq', 'fsdp'))
The draws below stay inside these ranges and needn't reach their ends.
Inputs may be any that keep to these rules, and one draw needn't show every extreme that they name: `decay_rate`: positive decay rates.
All inputs are finite; a program needn't handle non-finite values.
Results may differ from the reference program's by a relative error of at most 0.015.
The reference program's roundings to bfloat16 on the way (of `normed`, `mixed`, `normed_out`, `normed2` and `mid`) count: a program that leaves them out, or rounds other values in their place, can miss the bound.
Values may be sent and summed in bfloat16 or wider, within the bound.
A program may use at most 256 MiB of HBM per device.

```python
import math
import jax
import jax.numpy as jnp
from jax import lax

D = 1024
HEADS = 8
HEAD_K = 128
HEAD_V = 256
FF = 2816
CONV = 4
GROUP = 64
LENGTH = 512
BATCH = 8
KEY_DIM = 1024
VALUE_DIM = 2048


def draw_decay_rate(key, part):
    key = jax.random.fold_in(key, 7)
    lower = math.log(0.5 / LENGTH)
    upper = math.log(0.05)
    return jnp.exp(jax.random.uniform(key, (HEADS,), jnp.float32, lower, upper))


def level_of(key, dims, split, smallest, top_value):
    level, own = 1.0, jax.random.fold_in(key, 6)
    for position, shards_of in split:
        steps = jnp.exp(jax.random.uniform(jax.random.fold_in(own, position), (shards_of,), jnp.float32, smallest / len(split), top_value / len(split)))
        level = level * jnp.repeat(steps, dims[position] // shards_of).reshape([-1 if axis == position else 1 for axis in range(len(dims))])
    return level


def scatter_about(rng, dims, width, reach, shards=(), kind=jnp.bfloat16):
    factor_of = level_of(rng, dims, shards, -0.22, 0.18) if shards else 1.0
    values = jax.random.normal(rng, dims, jnp.float32) * width * factor_of
    return jnp.minimum(jnp.maximum(values, -reach), reach).astype(kind)


def setup_inputs(seed: int = 0) -> dict:
    seeds = jax.random.split(jax.random.key(seed), 21)
    return {
        "tokens": scatter_about(seeds[0], (BATCH, LENGTH, D), 1.0, 6.0, ((0, 8), (1, 4))),
        "attn_gain": jnp.clip(1.0 + 0.15 * jax.random.normal(seeds[1], (D,), jnp.float32), 0.25, 1.75),
        "w_query": scatter_about(seeds[2], (D, KEY_DIM), D ** -0.5, 0.1875, ((0, 32),)),
        "w_key": scatter_about(seeds[3], (D, KEY_DIM), D ** -0.5, 0.1875, ((0, 32),)),
        "value_weight": scatter_about(seeds[4], (D, VALUE_DIM), D ** -0.5, 0.1875, ((0, 32),)),
        "w_gate": scatter_about(seeds[5], (D, VALUE_DIM), D ** -0.5, 0.1875, ((0, 32),)),
        "w_beta": scatter_about(seeds[6], (D, HEADS), D ** -0.5, 0.1875, ((0, 32),)),
        "w_decay": scatter_about(seeds[7], (D, HEADS), D ** -0.5, 0.1875, ((0, 32),)),
        "conv_query": scatter_about(seeds[8], (CONV, KEY_DIM), 0.5, 2.0, (), jnp.float32),
        "conv_key": scatter_about(seeds[9], (CONV, KEY_DIM), 0.5, 2.0, (), jnp.float32),
        "conv_value": scatter_about(seeds[10], (CONV, VALUE_DIM), 0.5, 2.0, (), jnp.float32),
        "decay_rate": draw_decay_rate(jax.random.fold_in(seeds[20], 71), 0),
        "decay_bias": jnp.clip(jax.random.uniform(seeds[12], (HEADS,), jnp.float32, -1.0, 1.0), -1.0, 1.0),
        "out_gain": jnp.clip(1.0 + 0.15 * jax.random.normal(seeds[13], (HEAD_V,), jnp.float32), 0.25, 1.75),
        "w_out": scatter_about(seeds[14], (VALUE_DIM, D), VALUE_DIM ** -0.5, 0.125, ((0, 32),)),
        "mlp_gain": jnp.clip(1.0 + 0.15 * jax.random.normal(seeds[15], (D,), jnp.float32), 0.25, 1.75),
        "w_mlp_gate": scatter_about(seeds[16], (D, FF), D ** -0.5, 0.1875, ((0, 32),)),
        "w_up": scatter_about(seeds[17], (D, FF), D ** -0.5, 0.1875, ((0, 32),)),
        "w_down": scatter_about(seeds[18], (FF, D), FF ** -0.5, 0.109375, ((0, 32),)),
        "cotangent": scatter_about(seeds[19], (BATCH, LENGTH, D), 1.0, 6.0, ((0, 8), (1, 4))),
    }


epsilon = 1e-06
highest_precision = lax.Precision.HIGHEST

@jax.custom_vjp
def low(v):
    return lax.optimization_barrier(v.astype(jnp.bfloat16)).astype(jnp.float32)

@jax.custom_vjp
def low_back(v):
    return v

def low_keep(v):
    return (low(v), None)

def low_pass(kept, grad):
    return (grad,)

def back_keep(v):
    return (v, None)

def back_low(kept, grad):
    return (low(grad),)
low.defvjp(low_keep, low_pass)
low_back.defvjp(back_keep, back_low)

def matmul(left, right):
    return jnp.dot(left, right, precision=highest_precision)

def rms_scale(signal, gain):
    return signal * lax.rsqrt(lax.optimization_barrier(jnp.mean(signal * signal, axis=-1, keepdims=True)) + epsilon) * gain

def unit_rows(signal):
    return signal * lax.rsqrt(lax.optimization_barrier(jnp.sum(signal * signal, axis=-1, keepdims=True)) + epsilon)

def causal_conv(signal, kernel):
    length = signal.shape[-2]
    taps = kernel.shape[0]
    padding = [(0, 0)] * (signal.ndim - 2) + [(taps - 1, 0), (0, 0)]
    padded = jnp.pad(signal, padding)
    summed = jnp.zeros_like(signal)
    for offset in range(taps):
        summed = summed + kernel[offset] * lax.slice_in_dim(padded, offset, offset + length, axis=signal.ndim - 2)
    return summed

def delta_rule(queries, keys_all, values_all, strength, decay):
    steps = queries.shape[0]
    memory = jnp.zeros((queries.shape[1], queries.shape[2], values_all.shape[2]), queries.dtype)

    def one_token(carried_state, inputs):
        single_query_row, single_key_row, value_row, write, forget = inputs
        carried_state = forget[:, None, None] * carried_state
        recalled_value = jnp.einsum('az,azm->am', single_key_row, carried_state, precision=highest_precision)
        carried_state = carried_state + write[:, None, None] * single_key_row[:, :, None] * (value_row - recalled_value)[:, None, :]
        return (carried_state, jnp.einsum('az,azm->am', single_query_row, carried_state, precision=highest_precision))

    def one_block(carried_state, inputs):
        return lax.scan(one_token, carried_state, inputs)
    shaped = tuple((t.reshape((steps // GROUP, GROUP) + t.shape[1:]) for t in (queries, keys_all, values_all, strength, decay)))
    _, outputs = lax.scan(jax.checkpoint(one_block), memory, shaped)
    return outputs.reshape(steps, queries.shape[1], values_all.shape[2])

def forward(tokens, attn_gain, w_query, w_key, value_weight, w_gate, w_beta, w_decay, conv_query, conv_key, conv_value, decay_rate, decay_bias, out_gain, w_out, mlp_gain, w_mlp_gate, w_up, w_down):
    length = tokens.shape[0]
    normed = low(rms_scale(tokens, attn_gain))
    q_raw = low(low_back(matmul(normed, w_query)))
    k_raw = low(low_back(matmul(normed, w_key)))
    v_raw = low(low_back(matmul(normed, value_weight)))
    beta_raw = low(low_back(matmul(normed, w_beta)))
    decay_raw = low(low_back(matmul(normed, w_decay)))
    gate = low_back(matmul(normed, w_gate))
    queries = unit_rows(jax.nn.silu(causal_conv(q_raw, conv_query)).reshape(length, HEADS, HEAD_K)) * HEAD_K ** (-0.5)
    keys_all = unit_rows(jax.nn.silu(causal_conv(k_raw, conv_key)).reshape(length, HEADS, HEAD_K))
    values_all = jax.nn.silu(causal_conv(v_raw, conv_value)).reshape(length, HEADS, HEAD_V)
    strength = jax.nn.sigmoid(beta_raw)
    decay = jnp.exp(-decay_rate * jax.nn.softplus(decay_raw + decay_bias))
    mixed = low(low_back(delta_rule(queries, keys_all, values_all, strength, decay)))
    normed_out = rms_scale(mixed, out_gain) * jax.nn.silu(gate.reshape(length, HEADS, HEAD_V))
    hidden = tokens + low_back(matmul(low(normed_out.reshape(length, VALUE_DIM)), w_out))
    normed2 = low(rms_scale(hidden, mlp_gain))
    mlp_gate = low_back(matmul(normed2, w_mlp_gate))
    up_values = low_back(matmul(normed2, w_up))
    mid = low(jax.nn.silu(mlp_gate) * up_values)
    return hidden + matmul(mid, w_down)

def reference(tokens, attn_gain, w_query, w_key, value_weight, w_gate, w_beta, w_decay, conv_query, conv_key, conv_value, decay_rate, decay_bias, out_gain, w_out, mlp_gain, w_mlp_gate, w_up, w_down, cotangent):
    params = tuple((p.astype(jnp.float32) for p in (attn_gain, w_query, w_key, value_weight, w_gate, w_beta, w_decay, conv_query, conv_key, conv_value, decay_rate, decay_bias, out_gain, w_out, mlp_gain, w_mlp_gate, w_up, w_down)))

    def one_sequence(totals, pair):
        sequence, sequence_grad = pair
        result, pull = jax.vjp(forward, sequence.astype(jnp.float32), *params)
        grads = pull(sequence_grad.astype(jnp.float32))
        totals = tuple((t + g for t, g in zip(totals, grads[1:])))
        return (totals, (result.astype(jnp.bfloat16), grads[0]))
    zeros = tuple((jnp.zeros_like(p) for p in params))
    totals, (output, grad_tokens) = lax.scan(one_sequence, zeros, (tokens, cotangent))
    return (output, grad_tokens) + totals
```

```python
import jax
import jax.numpy as jnp
from jax import lax
from jax.experimental import pallas as pl
from jax.experimental.pallas import tpu as pltpu
from jax.sharding import PartitionSpec as P

CHUNK = 128


epsilon = 1e-06
highest_precision = lax.Precision.HIGHEST


def bf_dot(left, right):
    return jnp.dot(left, right, preferred_element_type=jnp.float32)


def rms_scale(signal, gain):
    return signal * lax.rsqrt(jnp.mean(signal * signal, axis=-1, keepdims=True) + epsilon) * gain


def unit_rows(signal):
    return signal * lax.rsqrt(jnp.sum(signal * signal, axis=-1, keepdims=True) + epsilon)


def contract(left, right, left_dim, right_dim):
    return lax.dot_general(
        left,
        right,
        (((left_dim,), (right_dim,)), ((), ())),
        precision=highest_precision,
        preferred_element_type=jnp.float32,
    )


@jax.custom_vjp
def mm(left, right):
    return contract(left, right, 1, 0)


@jax.custom_vjp
def mm_nt(left, right):
    return contract(left, right, 1, 1)


@jax.custom_vjp
def mm_tn(left, right):
    return contract(left, right, 0, 0)


mm.defvjp(
    lambda a, b: (contract(a, b, 1, 0), (a, b)),
    lambda kept, g: (contract(g, kept[1], 1, 1), contract(kept[0], g, 0, 0)),
)
mm_nt.defvjp(
    lambda a, b: (contract(a, b, 1, 1), (a, b)),
    lambda kept, g: (contract(g, kept[1], 1, 0), contract(g, kept[0], 0, 0)),
)
mm_tn.defvjp(
    lambda a, b: (contract(a, b, 0, 0), (a, b)),
    lambda kept, g: (contract(kept[1], g, 1, 1), contract(kept[0], g, 1, 0)),
)


def unit_lower_inverse(lower):
    size = lower.shape[0]
    row = lax.broadcasted_iota(jnp.int32, (size, size), 0)
    col = lax.broadcasted_iota(jnp.int32, (size, size), 1)
    inverse = jnp.where(row == col, 1.0, 0.0).astype(jnp.float32)
    level = 0
    while (1 << level) < size:
        row_block = lax.shift_right_logical(row, level)
        col_block = lax.shift_right_logical(col, level)
        part = jnp.where(
            (row_block == col_block + 1) & (jnp.bitwise_and(row_block, 1) == 1), lower, 0.0
        )
        if level == 0:
            inverse = inverse - part
        else:
            inverse = inverse - contract(contract(inverse, part, 1, 0), inverse, 1, 0)
        level += 1
    return inverse


@jax.custom_vjp
def known_inverse(lower, inverse):
    return inverse


known_inverse.defvjp(
    lambda lower, inverse: (inverse, inverse),
    lambda inverse, g: (
        -contract(contract(inverse, g, 0, 0), inverse, 1, 1),
        jnp.zeros_like(inverse),
    ),
)


def twice(wide, width):
    return jnp.concatenate([wide] * (width // wide.shape[1]), axis=1)


def chunk_step(memory, queries, keys, values, strength, log_decay, inverse=None):
    size = queries.shape[0]
    head_v = values.shape[1]
    row = lax.broadcasted_iota(jnp.int32, (size, size), 0)
    col = lax.broadcasted_iota(jnp.int32, (size, size), 1)
    causal = row >= col
    strict = row > col
    upto = jnp.where(causal, 1.0, 0.0).astype(jnp.float32)
    after = jnp.where(strict, 0.0, 1.0 - jnp.where(row == col, 1.0, 0.0)).astype(jnp.float32)
    pair = jnp.exp(mm(upto, jnp.where(strict, log_decay, 0.0)))
    lower = jnp.where(strict, strength * mm_nt(keys, keys) * pair, 0.0)
    if inverse is None:
        inverse = unit_lower_inverse(lower)
        solve = inverse
    else:
        solve = known_inverse(lower, inverse)
    from_start = jnp.exp(mm(upto, log_decay))
    to_end = jnp.exp(mm(after, log_decay))
    whole = jnp.exp(mm(jnp.ones_like(upto), log_decay))
    right_side = twice(strength, head_v) * values - mm(strength * from_start * keys, memory)
    corrected = mm(solve, right_side)
    scores = jnp.where(causal, mm_nt(queries, keys) * pair, 0.0)
    outputs = mm(from_start * queries, memory) + mm(scores, corrected)
    new_memory = twice(whole, head_v) * memory + mm_tn(keys * to_end, corrected)
    return new_memory, outputs, inverse


def forward_kernel(q_ref, k_ref, v_ref, s_ref, d_ref, out_ref, mem_ref, inv_ref, state):
    @pl.when(pl.program_id(0) == 0)
    def _():
        state[...] = jnp.zeros_like(state)

    for i in range(q_ref.shape[0]):
        memory = state[i]
        mem_ref[0, i] = memory
        new_memory, outputs, inverse = chunk_step(
            memory, q_ref[i], k_ref[i], v_ref[i], s_ref[i], d_ref[i]
        )
        state[i] = new_memory
        out_ref[i] = outputs
        inv_ref[0, i] = inverse


def backward_kernel(
    q_ref, k_ref, v_ref, s_ref, d_ref, mem_ref, inv_ref, g_ref,
    gq_ref, gk_ref, gv_ref, gs_ref, gd_ref, state,
):
    @pl.when(pl.program_id(0) == 0)
    def _():
        state[...] = jnp.zeros_like(state)

    for i in range(q_ref.shape[0]):
        inverse = inv_ref[0, i]

        def step(memory, q, k, v, s, d, inverse=inverse):
            return chunk_step(memory, q, k, v, s, d, inverse)[:2]

        _, pull = jax.vjp(
            step, mem_ref[0, i], q_ref[i], k_ref[i], v_ref[i], s_ref[i], d_ref[i]
        )
        gm, gq, gk, gv, gs, gd = pull((state[i], g_ref[i]))
        state[i] = gm
        gq_ref[i] = gq
        gk_ref[i] = gk
        gv_ref[i] = gv
        gs_ref[i] = gs
        gd_ref[i] = gd


def run_forward(queries, keys, values, strength, log_decay):
    streams, length, head_k = queries.shape
    head_v = values.shape[2]
    chunks = length // CHUNK
    narrow = pl.BlockSpec((streams, CHUNK, head_k), lambda c: (0, c, 0))
    wide = pl.BlockSpec((streams, CHUNK, head_v), lambda c: (0, c, 0))
    memories = pl.BlockSpec((1, streams, head_k, head_v), lambda c: (c, 0, 0, 0))
    inverses = pl.BlockSpec((1, streams, CHUNK, CHUNK), lambda c: (c, 0, 0, 0))
    return pl.pallas_call(
        forward_kernel,
        grid=(chunks,),
        in_specs=[narrow, narrow, wide, narrow, narrow],
        out_specs=[wide, memories, inverses],
        out_shape=[
            jax.ShapeDtypeStruct((streams, length, head_v), jnp.float32),
            jax.ShapeDtypeStruct((chunks, streams, head_k, head_v), jnp.float32),
            jax.ShapeDtypeStruct((chunks, streams, CHUNK, CHUNK), jnp.float32),
        ],
        scratch_shapes=[pltpu.VMEM((streams, head_k, head_v), jnp.float32)],
        compiler_params=pltpu.CompilerParams(vmem_limit_bytes=32 * 1024 * 1024),
        cost_estimate=pl.CostEstimate(
            flops=60_000_000 * chunks * streams, bytes_accessed=8_000_000, transcendentals=0
        ),
        name="recurrence_forward",
    )(queries, keys, values, strength, log_decay)


def run_backward(queries, keys, values, strength, log_decay, memory, inverse, grad):
    streams, length, head_k = queries.shape
    head_v = values.shape[2]
    chunks = length // CHUNK
    last = chunks - 1
    narrow = pl.BlockSpec((streams, CHUNK, head_k), lambda c: (0, last - c, 0))
    wide = pl.BlockSpec((streams, CHUNK, head_v), lambda c: (0, last - c, 0))
    memories = pl.BlockSpec((1, streams, head_k, head_v), lambda c: (last - c, 0, 0, 0))
    inverses = pl.BlockSpec((1, streams, CHUNK, CHUNK), lambda c: (last - c, 0, 0, 0))
    narrow_shape = jax.ShapeDtypeStruct((streams, length, head_k), jnp.float32)
    wide_shape = jax.ShapeDtypeStruct((streams, length, head_v), jnp.float32)
    return pl.pallas_call(
        backward_kernel,
        grid=(chunks,),
        in_specs=[narrow, narrow, wide, narrow, narrow, memories, inverses, wide],
        out_specs=[narrow, narrow, wide, narrow, narrow],
        out_shape=[narrow_shape, narrow_shape, wide_shape, narrow_shape, narrow_shape],
        scratch_shapes=[pltpu.VMEM((streams, head_k, head_v), jnp.float32)],
        compiler_params=pltpu.CompilerParams(vmem_limit_bytes=32 * 1024 * 1024),
        cost_estimate=pl.CostEstimate(
            flops=120_000_000 * chunks * streams, bytes_accessed=12_000_000, transcendentals=0
        ),
        name="recurrence_backward",
    )(queries, keys, values, strength, log_decay, memory, inverse, grad)


def prepare(moved, conv_q, conv_k, conv_v, rate, bias):
    batches, local, length, _ = moved.shape
    head_k = conv_q.shape[2]
    head_v = conv_v.shape[2]

    def conv(signal, kernel):
        taps = kernel.shape[0]
        padded = jnp.pad(signal, [(0, 0), (0, 0), (taps - 1, 0), (0, 0)])
        summed = jnp.zeros_like(signal)
        for offset in range(taps):
            summed = summed + kernel[offset][:, None, :] * lax.slice_in_dim(
                padded, offset, offset + length, axis=2
            )
        return summed

    edge = 2 * head_k + head_v
    queries = unit_rows(jax.nn.silu(conv(moved[..., :head_k], conv_q))) * head_k ** (-0.5)
    keys = unit_rows(jax.nn.silu(conv(moved[..., head_k : 2 * head_k], conv_k)))
    values = jax.nn.silu(conv(moved[..., 2 * head_k : edge], conv_v))
    strength = jax.nn.sigmoid(moved[..., edge : edge + 1])
    log_decay = -rate[:, None, None] * jax.nn.softplus(
        moved[..., edge + 1 : edge + 2] + bias[:, None, None]
    )
    shape = (batches * local, length)
    lanes = (batches, local, length, head_k)
    return (
        queries.reshape(shape + (head_k,)),
        keys.reshape(shape + (head_k,)),
        values.reshape(shape + (head_v,)),
        jnp.broadcast_to(strength, lanes).reshape(shape + (head_k,)),
        jnp.broadcast_to(log_decay, lanes).reshape(shape + (head_k,)),
    )


def to_heads(rows):
    count = lax.axis_size("seq")
    batches, positions, heads, width = rows.shape
    local = heads // count
    split = rows.reshape(batches, positions, count, local, width).transpose(2, 0, 3, 1, 4)
    moved = lax.all_to_all(split, "seq", split_axis=0, concat_axis=0, tiled=True)
    return moved.transpose(1, 2, 0, 3, 4).reshape(batches, local, count * positions, width)


def to_positions(by_head):
    count = lax.axis_size("seq")
    batches, local, length, width = by_head.shape
    positions = length // count
    split = by_head.reshape(batches, local, count, positions, width).transpose(2, 0, 1, 3, 4)
    moved = lax.all_to_all(split, "seq", split_axis=0, concat_axis=0, tiled=True)
    return moved.transpose(1, 3, 0, 2, 4).reshape(batches, positions, count * local, width)


def total_of(vector):
    for axis in ("fsdp", "seq"):
        size = lax.axis_size(axis)
        if size & (size - 1):
            vector = lax.psum(vector, axis)
            continue
        bit = 1
        while bit < size:
            vector = vector + lax.ppermute(vector, axis, [(i, i ^ bit) for i in range(size)])
            bit *= 2
    return vector


def total_small(parts):
    flat = jnp.concatenate([p.reshape(-1) for p in parts])
    count = flat.shape[0]
    padded = -(-count // 1024) * 1024
    summed = total_of(jnp.pad(flat, (0, padded - count)).reshape(-1, 128)).reshape(-1)
    results = []
    start = 0
    for p in parts:
        results.append(summed[start : start + p.size].reshape(p.shape))
        start += p.size
    return results


def gather(shard):
    return lax.all_gather(shard, ("seq", "fsdp"), axis=0, tiled=True)


def scatter(partial):
    return lax.psum_scatter(
        partial.astype(jnp.bfloat16), ("seq", "fsdp"), scatter_dimension=0, tiled=True
    ).astype(jnp.float32)


def out_piece(values, gate_values, gain):
    return rms_scale(values, gain) * jax.nn.silu(gate_values)


def swish_piece(gate_values, up_values):
    return jax.nn.silu(gate_values) * up_values


def widen(part, whole_shape, offset):
    return lax.dynamic_update_slice_in_dim(
        jnp.zeros(whole_shape, jnp.float32), part, offset, part.ndim - 1
    )


def column_term(left, right):
    return bf_dot(left.T, right)


def on_device(
    tokens,
    attn_gain,
    w_query,
    w_key,
    value_weight,
    w_gate,
    w_beta,
    w_decay,
    conv_query,
    conv_key,
    conv_value,
    decay_rate,
    decay_bias,
    out_gain,
    w_out,
    mlp_gain,
    w_mlp_gate,
    w_up,
    w_down,
    cotangent,
):
    batches, positions, width = tokens.shape
    head_count = w_beta.shape[1]
    key_dim = w_query.shape[1]
    value_dim = value_weight.shape[1]
    ff_width = w_mlp_gate.shape[1]
    head_k = key_dim // head_count
    head_v = value_dim // head_count
    row_count = batches * positions
    count = lax.axis_size("seq") * lax.axis_size("fsdp")
    out_rows = w_out.shape[0]
    down_rows = w_down.shape[0]
    edge_two = 2 * key_dim
    edge_three = edge_two + value_dim
    edge_four = edge_three + value_dim
    edge_five = edge_four + head_count
    edge_six = edge_five + head_count

    mixer_w = gather(
        jnp.concatenate([w_query, w_key, value_weight, w_gate, w_beta, w_decay], axis=1)
    )
    ffn_w = gather(jnp.concatenate([w_mlp_gate, w_up], axis=1))
    tall_w = gather(jnp.concatenate([w_out, w_down], axis=0)).reshape(
        count, out_rows + down_rows, width
    )
    who = tall_w[:, :out_rows].reshape(count * out_rows, width)
    whd = tall_w[:, out_rows:].reshape(count * down_rows, width)

    flattened = tokens.reshape(row_count, width).astype(jnp.float32)
    normed, pull_first = jax.vjp(rms_scale, flattened, attn_gain)
    normed_b = normed.astype(jnp.bfloat16)
    projected = bf_dot(normed_b, mixer_w)
    attn_gate = projected[:, edge_three:edge_four]

    def heads_of(columns, size):
        return columns.astype(jnp.bfloat16).reshape(batches, positions, head_count, size)

    logits = jnp.stack([projected[:, edge_four:edge_five], projected[:, edge_five:edge_six]], -1)
    rows = jnp.concatenate(
        [
            heads_of(projected[:, :key_dim], head_k),
            heads_of(projected[:, key_dim:edge_two], head_k),
            heads_of(projected[:, edge_two:edge_three], head_v),
            jnp.pad(heads_of(logits, 2), [(0, 0), (0, 0), (0, 0), (0, 126)]),
        ],
        axis=-1,
    )
    moved = to_heads(rows).astype(jnp.float32)
    local = head_count // lax.axis_size("seq")
    first = lax.axis_index("seq") * local

    def local_taps(kernel, size):
        part = lax.dynamic_slice_in_dim(kernel, first * size, local * size, 1)
        return part.reshape(kernel.shape[0], local, size)

    rate_local = lax.dynamic_slice_in_dim(decay_rate, first, local, 0)
    bias_local = lax.dynamic_slice_in_dim(decay_bias, first, local, 0)
    prepared, pull_prepare = jax.vjp(
        prepare,
        moved,
        local_taps(conv_query, head_k),
        local_taps(conv_key, head_k),
        local_taps(conv_value, head_v),
        rate_local,
        bias_local,
    )
    length = moved.shape[2]
    mixed, memories, inverses = run_forward(*prepared)
    returned = to_positions(
        mixed.astype(jnp.bfloat16).reshape(batches, local, length, head_v)
    )
    gate_heads = attn_gate.reshape(row_count, head_count, head_v)
    normed_out, pull_out = jax.vjp(
        out_piece,
        returned.reshape(row_count, head_count, head_v).astype(jnp.float32),
        gate_heads,
        out_gain,
    )
    normed_out_b = normed_out.reshape(row_count, value_dim).astype(jnp.bfloat16)
    hidden = flattened + bf_dot(normed_out_b, who)
    normed2, pull_second = jax.vjp(rms_scale, hidden, mlp_gain)
    normed2_b = normed2.astype(jnp.bfloat16)
    mlp_both = bf_dot(normed2_b, ffn_w)
    mid, pull_mid = jax.vjp(swish_piece, mlp_both[:, :ff_width], mlp_both[:, ff_width:])
    mid_b = mid.astype(jnp.bfloat16)
    result = (hidden + bf_dot(mid_b, whd)).astype(jnp.bfloat16).reshape(tokens.shape)
    grad_out_b = cotangent.reshape(row_count, width)
    grad_out = grad_out_b.astype(jnp.float32)
    grad_mid = bf_dot(grad_out_b, whd.T)
    grad_gate_m, grad_up_m = pull_mid(grad_mid)
    ffn_grads = jnp.concatenate(
        [grad_gate_m.astype(jnp.bfloat16), grad_up_m.astype(jnp.bfloat16)], axis=1
    )
    grad_normed2 = bf_dot(ffn_grads, ffn_w.T)
    grad_hidden_part, grad_mlp_gain = pull_second(grad_normed2)
    grad_hidden = grad_out + grad_hidden_part
    grad_hidden_b = grad_hidden.astype(jnp.bfloat16)
    grad_normed_out = bf_dot(grad_hidden_b, who.T).reshape(row_count, head_count, head_v)
    grad_returned, grad_gate_heads, grad_out_gain = pull_out(grad_normed_out)
    grad_mixed = to_heads(
        grad_returned.astype(jnp.bfloat16).reshape(batches, positions, head_count, head_v)
    )
    ffn_sum = scatter(column_term(normed2_b, ffn_grads))
    tall_sum = scatter(
        jnp.concatenate(
            [
                column_term(normed_out_b, grad_hidden_b).astype(jnp.bfloat16).reshape(
                    count, out_rows, width
                ),
                column_term(mid_b, grad_out_b).astype(jnp.bfloat16).reshape(
                    count, down_rows, width
                ),
            ],
            axis=1,
        ).reshape(count * (out_rows + down_rows), width)
    )
    prepared_grads = run_backward(
        *prepared,
        memories,
        inverses,
        grad_mixed.astype(jnp.float32).reshape(batches * local, length, head_v),
    )
    grad_moved, grad_cq, grad_ck, grad_cv, grad_rate, bias_gradient = pull_prepare(
        tuple(prepared_grads)
    )
    back = to_positions(grad_moved.astype(jnp.bfloat16)).reshape(row_count, head_count, -1)
    edge = 2 * head_k + head_v
    grad_gate_b = grad_gate_heads.reshape(row_count, value_dim).astype(jnp.bfloat16)
    mixer_grads = jnp.concatenate(
        [
            back[:, :, :head_k].reshape(row_count, key_dim),
            back[:, :, head_k : 2 * head_k].reshape(row_count, key_dim),
            back[:, :, 2 * head_k : edge].reshape(row_count, value_dim),
            grad_gate_b,
            back[:, :, edge],
            back[:, :, edge + 1],
        ],
        axis=1,
    )
    mixer_sum = scatter(column_term(normed_b, mixer_grads))
    normed_gradient = bf_dot(mixer_grads, mixer_w.T)
    grad_flat, grad_attn_gain = pull_first(normed_gradient)
    grad_tokens = (grad_flat + grad_hidden).reshape(tokens.shape)

    def flat_taps(grad):
        return grad.reshape(grad.shape[0], -1)

    small = total_small(
        (
            grad_attn_gain,
            grad_out_gain,
            grad_mlp_gain,
            widen(flat_taps(grad_cq), conv_query.shape, first * head_k),
            widen(flat_taps(grad_ck), conv_key.shape, first * head_k),
            widen(flat_taps(grad_cv), conv_value.shape, first * head_v),
            widen(grad_rate, decay_rate.shape, first),
            widen(bias_gradient, decay_bias.shape, first),
        )
    )
    sum_attn, sum_out_gain, sum_mlp_gain, sum_cq, sum_ck, sum_cv, sum_rate, sum_bias = small
    return (
        result,
        grad_tokens,
        sum_attn,
        mixer_sum[:, :key_dim],
        mixer_sum[:, key_dim:edge_two],
        mixer_sum[:, edge_two:edge_three],
        mixer_sum[:, edge_three:edge_four],
        mixer_sum[:, edge_four:edge_five],
        mixer_sum[:, edge_five:],
        sum_cq,
        sum_ck,
        sum_cv,
        sum_rate,
        sum_bias,
        sum_out_gain,
        tall_sum[:out_rows],
        sum_mlp_gain,
        ffn_sum[:, :ff_width],
        ffn_sum[:, ff_width:],
        tall_sum[out_rows:],
    )


def solution(mesh):
    in_specs = (
        P("fsdp", "seq", None),
        P(),
        P(("seq", "fsdp"), None),
        P(("seq", "fsdp"), None),
        P(("seq", "fsdp"), None),
        P(("seq", "fsdp"), None),
        P(("seq", "fsdp"), None),
        P(("seq", "fsdp"), None),
        P(),
        P(),
        P(),
        P(),
        P(),
        P(),
        P(("seq", "fsdp"), None),
        P(),
        P(("seq", "fsdp"), None),
        P(("seq", "fsdp"), None),
        P(("seq", "fsdp"), None),
        P("fsdp", "seq", None),
    )
    out_specs = (
        P("fsdp", "seq", None),
        P("fsdp", "seq", None),
        P(),
        P(("seq", "fsdp"), None),
        P(("seq", "fsdp"), None),
        P(("seq", "fsdp"), None),
        P(("seq", "fsdp"), None),
        P(("seq", "fsdp"), None),
        P(("seq", "fsdp"), None),
        P(),
        P(),
        P(),
        P(),
        P(),
        P(),
        P(("seq", "fsdp"), None),
        P(),
        P(("seq", "fsdp"), None),
        P(("seq", "fsdp"), None),
        P(("seq", "fsdp"), None),
    )
    return jax.shard_map(
        on_device, mesh=mesh, in_specs=in_specs, out_specs=out_specs, check_vma=False
    )
```

```python
import jax
import jax.numpy as jnp
from jax import lax
from jax.experimental import pallas as pl
from jax.experimental.pallas import tpu as pltpu
from jax.sharding import PartitionSpec as P

CHUNK = 128


epsilon = 1e-06
highest_precision = lax.Precision.HIGHEST


def bf_dot(left, right):
    return jnp.dot(left, right, preferred_element_type=jnp.float32)


def rms_scale(signal, gain):
    return signal * lax.rsqrt(jnp.mean(signal * signal, axis=-1, keepdims=True) + epsilon) * gain


def unit_rows(signal):
    return signal * lax.rsqrt(jnp.sum(signal * signal, axis=-1, keepdims=True) + epsilon)


def contract(left, right, left_dim, right_dim):
    return lax.dot_general(
        left,
        right,
        (((left_dim,), (right_dim,)), ((), ())),
        precision=highest_precision,
        preferred_element_type=jnp.float32,
    )


@jax.custom_vjp
def mm(left, right):
    return contract(left, right, 1, 0)


@jax.custom_vjp
def mm_nt(left, right):
    return contract(left, right, 1, 1)


@jax.custom_vjp
def mm_tn(left, right):
    return contract(left, right, 0, 0)


mm.defvjp(
    lambda a, b: (contract(a, b, 1, 0), (a, b)),
    lambda kept, g: (contract(g, kept[1], 1, 1), contract(kept[0], g, 0, 0)),
)
mm_nt.defvjp(
    lambda a, b: (contract(a, b, 1, 1), (a, b)),
    lambda kept, g: (contract(g, kept[1], 1, 0), contract(g, kept[0], 0, 0)),
)
mm_tn.defvjp(
    lambda a, b: (contract(a, b, 0, 0), (a, b)),
    lambda kept, g: (contract(kept[1], g, 1, 1), contract(kept[0], g, 1, 0)),
)


def unit_lower_inverse(lower):
    size = lower.shape[0]
    row = lax.broadcasted_iota(jnp.int32, (size, size), 0)
    col = lax.broadcasted_iota(jnp.int32, (size, size), 1)
    inverse = jnp.where(row == col, 1.0, 0.0).astype(jnp.float32)
    level = 0
    while (1 << level) < size:
        row_block = lax.shift_right_logical(row, level)
        col_block = lax.shift_right_logical(col, level)
        part = jnp.where(
            (row_block == col_block + 1) & (jnp.bitwise_and(row_block, 1) == 1), lower, 0.0
        )
        if level == 0:
            inverse = inverse - part
        else:
            inverse = inverse - contract(contract(inverse, part, 1, 0), inverse, 1, 0)
        level += 1
    return inverse


@jax.custom_vjp
def known_inverse(lower, inverse):
    return inverse


known_inverse.defvjp(
    lambda lower, inverse: (inverse, inverse),
    lambda inverse, g: (
        -contract(contract(inverse, g, 0, 0), inverse, 1, 1),
        jnp.zeros_like(inverse),
    ),
)


def twice(wide, width):
    return jnp.concatenate([wide] * (width // wide.shape[1]), axis=1)


def chunk_step(memory, queries, keys, values, strength, log_decay, inverse=None):
    size = queries.shape[0]
    head_v = values.shape[1]
    row = lax.broadcasted_iota(jnp.int32, (size, size), 0)
    col = lax.broadcasted_iota(jnp.int32, (size, size), 1)
    causal = row >= col
    strict = row > col
    upto = jnp.where(causal, 1.0, 0.0).astype(jnp.float32)
    after = jnp.where(strict, 0.0, 1.0 - jnp.where(row == col, 1.0, 0.0)).astype(jnp.float32)
    pair = jnp.exp(mm(upto, jnp.where(strict, log_decay, 0.0)))
    lower = jnp.where(strict, strength * mm_nt(keys, keys) * pair, 0.0)
    if inverse is None:
        inverse = unit_lower_inverse(lower)
        solve = inverse
    else:
        solve = known_inverse(lower, inverse)
    from_start = jnp.exp(mm(upto, log_decay))
    to_end = jnp.exp(mm(after, log_decay))
    whole = jnp.exp(mm(jnp.ones_like(upto), log_decay))
    right_side = twice(strength, head_v) * values - mm(strength * from_start * keys, memory)
    corrected = mm(solve, right_side)
    scores = jnp.where(causal, mm_nt(queries, keys) * pair, 0.0)
    outputs = mm(from_start * queries, memory) + mm(scores, corrected)
    new_memory = twice(whole, head_v) * memory + mm_tn(keys * to_end, corrected)
    return new_memory, outputs, inverse


def forward_kernel(q_ref, k_ref, v_ref, s_ref, d_ref, out_ref, mem_ref, inv_ref, state):
    @pl.when(pl.program_id(0) == 0)
    def _():
        state[...] = jnp.zeros_like(state)

    for i in range(q_ref.shape[0]):
        memory = state[i]
        mem_ref[0, i] = memory
        new_memory, outputs, inverse = chunk_step(
            memory, q_ref[i], k_ref[i], v_ref[i], s_ref[i], d_ref[i]
        )
        state[i] = new_memory
        out_ref[i] = outputs
        inv_ref[0, i] = inverse


def backward_kernel(
    q_ref, k_ref, v_ref, s_ref, d_ref, mem_ref, inv_ref, g_ref,
    gq_ref, gk_ref, gv_ref, gs_ref, gd_ref, state,
):
    @pl.when(pl.program_id(0) == 0)
    def _():
        state[...] = jnp.zeros_like(state)

    for i in range(q_ref.shape[0]):
        inverse = inv_ref[0, i]

        def step(memory, q, k, v, s, d, inverse=inverse):
            return chunk_step(memory, q, k, v, s, d, inverse)[:2]

        _, pull = jax.vjp(
            step, mem_ref[0, i], q_ref[i], k_ref[i], v_ref[i], s_ref[i], d_ref[i]
        )
        gm, gq, gk, gv, gs, gd = pull((state[i], g_ref[i]))
        state[i] = gm
        gq_ref[i] = gq
        gk_ref[i] = gk
        gv_ref[i] = gv
        gs_ref[i] = gs
        gd_ref[i] = gd


def run_forward(queries, keys, values, strength, log_decay):
    streams, length, head_k = queries.shape
    head_v = values.shape[2]
    chunks = length // CHUNK
    narrow = pl.BlockSpec((streams, CHUNK, head_k), lambda c: (0, c, 0))
    wide = pl.BlockSpec((streams, CHUNK, head_v), lambda c: (0, c, 0))
    memories = pl.BlockSpec((1, streams, head_k, head_v), lambda c: (c, 0, 0, 0))
    inverses = pl.BlockSpec((1, streams, CHUNK, CHUNK), lambda c: (c, 0, 0, 0))
    return pl.pallas_call(
        forward_kernel,
        grid=(chunks,),
        in_specs=[narrow, narrow, wide, narrow, narrow],
        out_specs=[wide, memories, inverses],
        out_shape=[
            jax.ShapeDtypeStruct((streams, length, head_v), jnp.float32),
            jax.ShapeDtypeStruct((chunks, streams, head_k, head_v), jnp.float32),
            jax.ShapeDtypeStruct((chunks, streams, CHUNK, CHUNK), jnp.float32),
        ],
        scratch_shapes=[pltpu.VMEM((streams, head_k, head_v), jnp.float32)],
        compiler_params=pltpu.CompilerParams(vmem_limit_bytes=32 * 1024 * 1024),
        cost_estimate=pl.CostEstimate(
            flops=60_000_000 * chunks * streams, bytes_accessed=8_000_000, transcendentals=0
        ),
        name="recurrence_forward",
    )(queries, keys, values, strength, log_decay)


def run_backward(queries, keys, values, strength, log_decay, memory, inverse, grad):
    streams, length, head_k = queries.shape
    head_v = values.shape[2]
    chunks = length // CHUNK
    last = chunks - 1
    narrow = pl.BlockSpec((streams, CHUNK, head_k), lambda c: (0, last - c, 0))
    wide = pl.BlockSpec((streams, CHUNK, head_v), lambda c: (0, last - c, 0))
    memories = pl.BlockSpec((1, streams, head_k, head_v), lambda c: (last - c, 0, 0, 0))
    inverses = pl.BlockSpec((1, streams, CHUNK, CHUNK), lambda c: (last - c, 0, 0, 0))
    narrow_shape = jax.ShapeDtypeStruct((streams, length, head_k), jnp.float32)
    wide_shape = jax.ShapeDtypeStruct((streams, length, head_v), jnp.float32)
    return pl.pallas_call(
        backward_kernel,
        grid=(chunks,),
        in_specs=[narrow, narrow, wide, narrow, narrow, memories, inverses, wide],
        out_specs=[narrow, narrow, wide, narrow, narrow],
        out_shape=[narrow_shape, narrow_shape, wide_shape, narrow_shape, narrow_shape],
        scratch_shapes=[pltpu.VMEM((streams, head_k, head_v), jnp.float32)],
        compiler_params=pltpu.CompilerParams(vmem_limit_bytes=32 * 1024 * 1024),
        cost_estimate=pl.CostEstimate(
            flops=120_000_000 * chunks * streams, bytes_accessed=12_000_000, transcendentals=0
        ),
        name="recurrence_backward",
    )(queries, keys, values, strength, log_decay, memory, inverse, grad)


def prepare(moved, conv_q, conv_k, conv_v, rate, bias):
    batches, local, length, _ = moved.shape
    head_k = conv_q.shape[2]
    head_v = conv_v.shape[2]

    def conv(signal, kernel):
        taps = kernel.shape[0]
        padded = jnp.pad(signal, [(0, 0), (0, 0), (taps - 1, 0), (0, 0)])
        summed = jnp.zeros_like(signal)
        for offset in range(taps):
            summed = summed + kernel[offset][:, None, :] * lax.slice_in_dim(
                padded, offset, offset + length, axis=2
            )
        return summed

    edge = 2 * head_k + head_v
    queries = unit_rows(jax.nn.silu(conv(moved[..., :head_k], conv_q))) * head_k ** (-0.5)
    keys = unit_rows(jax.nn.silu(conv(moved[..., head_k : 2 * head_k], conv_k)))
    values = jax.nn.silu(conv(moved[..., 2 * head_k : edge], conv_v))
    strength = jax.nn.sigmoid(moved[..., edge : edge + 1])
    log_decay = -rate[:, None, None] * jax.nn.softplus(
        moved[..., edge + 1 : edge + 2] + bias[:, None, None]
    )
    shape = (batches * local, length)
    lanes = (batches, local, length, head_k)
    return (
        queries.reshape(shape + (head_k,)),
        keys.reshape(shape + (head_k,)),
        values.reshape(shape + (head_v,)),
        jnp.broadcast_to(strength, lanes).reshape(shape + (head_k,)),
        jnp.broadcast_to(log_decay, lanes).reshape(shape + (head_k,)),
    )


def to_heads(rows):
    count = lax.axis_size("seq")
    batches, positions, heads, width = rows.shape
    local = heads // count
    split = rows.reshape(batches, positions, count, local, width).transpose(2, 0, 3, 1, 4)
    moved = lax.all_to_all(split, "seq", split_axis=0, concat_axis=0, tiled=True)
    return moved.transpose(1, 2, 0, 3, 4).reshape(batches, local, count * positions, width)


def to_positions(by_head):
    count = lax.axis_size("seq")
    batches, local, length, width = by_head.shape
    positions = length // count
    split = by_head.reshape(batches, local, count, positions, width).transpose(2, 0, 1, 3, 4)
    moved = lax.all_to_all(split, "seq", split_axis=0, concat_axis=0, tiled=True)
    return moved.transpose(1, 3, 0, 2, 4).reshape(batches, positions, count * local, width)


def total_of(vector):
    for axis in ("fsdp", "seq"):
        size = lax.axis_size(axis)
        if size & (size - 1):
            vector = lax.psum(vector, axis)
            continue
        bit = 1
        while bit < size:
            vector = vector + lax.ppermute(vector, axis, [(i, i ^ bit) for i in range(size)])
            bit *= 2
    return vector


def total_small(parts):
    flat = jnp.concatenate([p.reshape(-1) for p in parts])
    count = flat.shape[0]
    padded = -(-count // 1024) * 1024
    summed = total_of(jnp.pad(flat, (0, padded - count)).reshape(-1, 128)).reshape(-1)
    results = []
    start = 0
    for p in parts:
        results.append(summed[start : start + p.size].reshape(p.shape))
        start += p.size
    return results


def gather(shard):
    return lax.all_gather(shard, ("seq", "fsdp"), axis=0, tiled=True)


def mesh_bits():
    seq, fsdp = lax.axis_size("seq"), lax.axis_size("fsdp")
    seq_bits = [("seq", 1 << b) for b in range(seq.bit_length() - 1)]
    fsdp_bits = [("fsdp", 1 << b) for b in range(fsdp.bit_length() - 1)]
    return seq_bits, fsdp_bits


def halving_order(kind):
    seq_bits, fsdp_bits = mesh_bits()
    far = fsdp_bits[1:]
    if kind == 0:
        return seq_bits + far
    if kind == 1:
        return seq_bits[1:] + far + seq_bits[:1]
    return far[:1] + seq_bits + far[1:]


def swap(part, axis, bit):
    return lax.ppermute(part, axis, [(i, i ^ bit) for i in range(lax.axis_size(axis))])


def summed_term(left, right, kind):
    seq, fsdp = lax.axis_size("seq"), lax.axis_size("fsdp")
    count = seq * fsdp
    if seq & (seq - 1) or fsdp & (fsdp - 1) or fsdp < 2:
        return lax.psum_scatter(
            column_term(left, right), ("seq", "fsdp"), scatter_dimension=0, tiled=True
        )
    rows = left.shape[1] // count
    columns = right.shape[1]
    paired = left.reshape(left.shape[0], count // 2, 2, rows)
    core = lax.axis_index("fsdp") % 2

    def half(which):
        chosen = lax.dynamic_index_in_dim(paired, which, 2, keepdims=False)
        return column_term(chosen.reshape(left.shape[0], count // 2 * rows), right)

    arrived = swap(half(1 - core).astype(jnp.bfloat16), "fsdp", 1)
    total = half(core) + arrived.astype(jnp.float32)
    seq_bits, fsdp_bits = mesh_bits()
    live = seq_bits[::-1] + fsdp_bits[:0:-1]
    for axis, bit in halving_order(kind):
        place = live.index((axis, bit))
        before, after = 1 << place, 1 << (len(live) - 1 - place)
        split = total.astype(jnp.bfloat16).reshape(before, 2, after * rows, columns)
        mine = (lax.axis_index(axis) // bit) % 2
        keep = lax.dynamic_index_in_dim(split, mine, 1, keepdims=False)
        send = lax.dynamic_index_in_dim(split, 1 - mine, 1, keepdims=False)
        total = keep.astype(jnp.float32) + swap(send, axis, bit).astype(jnp.float32)
        live.remove((axis, bit))
    return total.reshape(rows, columns)


def out_piece(values, gate_values, gain):
    return rms_scale(values, gain) * jax.nn.silu(gate_values)


def swish_piece(gate_values, up_values):
    return jax.nn.silu(gate_values) * up_values


def widen(part, whole_shape, offset):
    return lax.dynamic_update_slice_in_dim(
        jnp.zeros(whole_shape, jnp.float32), part, offset, part.ndim - 1
    )


def column_term(left, right):
    return bf_dot(left.T, right)


def on_device(
    tokens,
    attn_gain,
    w_query,
    w_key,
    value_weight,
    w_gate,
    w_beta,
    w_decay,
    conv_query,
    conv_key,
    conv_value,
    decay_rate,
    decay_bias,
    out_gain,
    w_out,
    mlp_gain,
    w_mlp_gate,
    w_up,
    w_down,
    cotangent,
):
    batches, positions, width = tokens.shape
    head_count = w_beta.shape[1]
    key_dim = w_query.shape[1]
    value_dim = value_weight.shape[1]
    ff_width = w_mlp_gate.shape[1]
    head_k = key_dim // head_count
    head_v = value_dim // head_count
    row_count = batches * positions
    count = lax.axis_size("seq") * lax.axis_size("fsdp")
    out_rows = w_out.shape[0]
    down_rows = w_down.shape[0]
    edge_two = 2 * key_dim
    edge_three = edge_two + value_dim
    edge_four = edge_three + value_dim
    edge_five = edge_four + head_count
    edge_six = edge_five + head_count

    mixer_w = gather(
        jnp.concatenate([w_query, w_key, value_weight, w_gate, w_beta, w_decay], axis=1)
    )
    ffn_w = gather(jnp.concatenate([w_mlp_gate, w_up], axis=1))
    tall_w = gather(jnp.concatenate([w_out, w_down], axis=0)).reshape(
        count, out_rows + down_rows, width
    )
    who = tall_w[:, :out_rows].reshape(count * out_rows, width)
    whd = tall_w[:, out_rows:].reshape(count * down_rows, width)

    flattened = tokens.reshape(row_count, width).astype(jnp.float32)
    normed, pull_first = jax.vjp(rms_scale, flattened, attn_gain)
    normed_b = normed.astype(jnp.bfloat16)
    projected = bf_dot(normed_b, mixer_w)
    attn_gate = projected[:, edge_three:edge_four]

    def heads_of(columns, size):
        return columns.astype(jnp.bfloat16).reshape(batches, positions, head_count, size)

    logits = jnp.stack([projected[:, edge_four:edge_five], projected[:, edge_five:edge_six]], -1)
    rows = jnp.concatenate(
        [
            heads_of(projected[:, :key_dim], head_k),
            heads_of(projected[:, key_dim:edge_two], head_k),
            heads_of(projected[:, edge_two:edge_three], head_v),
            jnp.pad(heads_of(logits, 2), [(0, 0), (0, 0), (0, 0), (0, 126)]),
        ],
        axis=-1,
    )
    moved = to_heads(rows).astype(jnp.float32)
    local = head_count // lax.axis_size("seq")
    first = lax.axis_index("seq") * local

    def local_taps(kernel, size):
        part = lax.dynamic_slice_in_dim(kernel, first * size, local * size, 1)
        return part.reshape(kernel.shape[0], local, size)

    rate_local = lax.dynamic_slice_in_dim(decay_rate, first, local, 0)
    bias_local = lax.dynamic_slice_in_dim(decay_bias, first, local, 0)
    prepared, pull_prepare = jax.vjp(
        prepare,
        moved,
        local_taps(conv_query, head_k),
        local_taps(conv_key, head_k),
        local_taps(conv_value, head_v),
        rate_local,
        bias_local,
    )
    length = moved.shape[2]
    mixed, memories, inverses = run_forward(*prepared)
    returned = to_positions(
        mixed.astype(jnp.bfloat16).reshape(batches, local, length, head_v)
    )
    gate_heads = attn_gate.reshape(row_count, head_count, head_v)
    normed_out, pull_out = jax.vjp(
        out_piece,
        returned.reshape(row_count, head_count, head_v).astype(jnp.float32),
        gate_heads,
        out_gain,
    )
    normed_out_b = normed_out.reshape(row_count, value_dim).astype(jnp.bfloat16)
    hidden = flattened + bf_dot(normed_out_b, who)
    normed2, pull_second = jax.vjp(rms_scale, hidden, mlp_gain)
    normed2_b = normed2.astype(jnp.bfloat16)
    mlp_both = bf_dot(normed2_b, ffn_w)
    mid, pull_mid = jax.vjp(swish_piece, mlp_both[:, :ff_width], mlp_both[:, ff_width:])
    mid_b = mid.astype(jnp.bfloat16)
    result = (hidden + bf_dot(mid_b, whd)).astype(jnp.bfloat16).reshape(tokens.shape)
    grad_out_b = cotangent.reshape(row_count, width)
    grad_out = grad_out_b.astype(jnp.float32)
    grad_mid = bf_dot(grad_out_b, whd.T)
    grad_gate_m, grad_up_m = pull_mid(grad_mid)
    ffn_grads = jnp.concatenate(
        [grad_gate_m.astype(jnp.bfloat16), grad_up_m.astype(jnp.bfloat16)], axis=1
    )
    grad_normed2 = bf_dot(ffn_grads, ffn_w.T)
    grad_hidden_part, grad_mlp_gain = pull_second(grad_normed2)
    grad_hidden = grad_out + grad_hidden_part
    grad_hidden_b = grad_hidden.astype(jnp.bfloat16)
    grad_normed_out = bf_dot(grad_hidden_b, who.T).reshape(row_count, head_count, head_v)
    grad_returned, grad_gate_heads, grad_out_gain = pull_out(grad_normed_out)
    grad_mixed = to_heads(
        grad_returned.astype(jnp.bfloat16).reshape(batches, positions, head_count, head_v)
    )
    down_sum = summed_term(mid_b, grad_out_b, 0)
    sum_wm = summed_term(normed2_b, ffn_grads[:, :ff_width], 1)
    sum_wu = summed_term(normed2_b, ffn_grads[:, ff_width:], 2)
    out_sum = summed_term(normed_out_b, grad_hidden_b, 0)
    grad_gate_b = grad_gate_heads.reshape(row_count, value_dim).astype(jnp.bfloat16)
    sum_wg = summed_term(normed_b, grad_gate_b, 1)
    prepared_grads = run_backward(
        *prepared,
        memories,
        inverses,
        grad_mixed.astype(jnp.float32).reshape(batches * local, length, head_v),
    )
    grad_moved, grad_cq, grad_ck, grad_cv, grad_rate, bias_gradient = pull_prepare(
        tuple(prepared_grads)
    )
    back = to_positions(grad_moved.astype(jnp.bfloat16)).reshape(row_count, head_count, -1)
    edge = 2 * head_k + head_v
    mixer_grads = jnp.concatenate(
        [
            back[:, :, :head_k].reshape(row_count, key_dim),
            back[:, :, head_k : 2 * head_k].reshape(row_count, key_dim),
            back[:, :, 2 * head_k : edge].reshape(row_count, value_dim),
            grad_gate_b,
            back[:, :, edge],
            back[:, :, edge + 1],
        ],
        axis=1,
    )
    third = edge_three // 384 * 128
    logit_grads = jnp.concatenate([back[:, :, edge], back[:, :, edge + 1]], axis=1)
    qkv_sum = jnp.concatenate(
        [
            summed_term(normed_b, mixer_grads[:, :third], 0),
            summed_term(normed_b, mixer_grads[:, third : 2 * third], 1),
            summed_term(
                normed_b,
                jnp.concatenate([mixer_grads[:, 2 * third : edge_three], logit_grads], axis=1),
                2,
            ),
        ],
        axis=1,
    )
    normed_gradient = bf_dot(mixer_grads, mixer_w.T)
    grad_flat, grad_attn_gain = pull_first(normed_gradient)
    grad_tokens = (grad_flat + grad_hidden).reshape(tokens.shape)

    def flat_taps(grad):
        return grad.reshape(grad.shape[0], -1)

    small = total_small(
        (
            grad_attn_gain,
            grad_out_gain,
            grad_mlp_gain,
            widen(flat_taps(grad_cq), conv_query.shape, first * head_k),
            widen(flat_taps(grad_ck), conv_key.shape, first * head_k),
            widen(flat_taps(grad_cv), conv_value.shape, first * head_v),
            widen(grad_rate, decay_rate.shape, first),
            widen(bias_gradient, decay_bias.shape, first),
        )
    )
    sum_attn, sum_out_gain, sum_mlp_gain, sum_cq, sum_ck, sum_cv, sum_rate, sum_bias = small
    return (
        result,
        grad_tokens,
        sum_attn,
        qkv_sum[:, :key_dim],
        qkv_sum[:, key_dim:edge_two],
        qkv_sum[:, edge_two:edge_three],
        sum_wg,
        qkv_sum[:, edge_three : edge_three + head_count],
        qkv_sum[:, edge_three + head_count :],
        sum_cq,
        sum_ck,
        sum_cv,
        sum_rate,
        sum_bias,
        sum_out_gain,
        out_sum,
        sum_mlp_gain,
        sum_wm,
        sum_wu,
        down_sum,
    )


def solution(mesh):
    in_specs = (
        P("fsdp", "seq", None),
        P(),
        P(("seq", "fsdp"), None),
        P(("seq", "fsdp"), None),
        P(("seq", "fsdp"), None),
        P(("seq", "fsdp"), None),
        P(("seq", "fsdp"), None),
        P(("seq", "fsdp"), None),
        P(),
        P(),
        P(),
        P(),
        P(),
        P(),
        P(("seq", "fsdp"), None),
        P(),
        P(("seq", "fsdp"), None),
        P(("seq", "fsdp"), None),
        P(("seq", "fsdp"), None),
        P("fsdp", "seq", None),
    )
    out_specs = (
        P("fsdp", "seq", None),
        P("fsdp", "seq", None),
        P(),
        P(("seq", "fsdp"), None),
        P(("seq", "fsdp"), None),
        P(("seq", "fsdp"), None),
        P(("seq", "fsdp"), None),
        P(("seq", "fsdp"), None),
        P(("seq", "fsdp"), None),
        P(),
        P(),
        P(),
        P(),
        P(),
        P(),
        P(("seq", "fsdp"), None),
        P(),
        P(("seq", "fsdp"), None),
        P(("seq", "fsdp"), None),
        P(("seq", "fsdp"), None),
    )
    return jax.shard_map(
        on_device, mesh=mesh, in_specs=in_specs, out_specs=out_specs, check_vma=False
    )
```
